32 devices in a mesh: dp: 8 (over z, y), seq: 4 (over x, core).
Axes of the slice: x: 2, y: 2, z: 4, core: 2. Of those that a mesh axis runs over, the one named last changes fastest.
Arguments:
- inputs: bfloat16 [16, 2048, 768], P('dp', 'seq'), may hold values from -6 to 6
- conv_weight: bfloat16 [3, 768, 384], P(None, 'dp', 'seq'), may hold values from -0.125 to 0.125
- point_weight: bfloat16 [384, 768], P('seq', 'dp'), may hold values from -0.3125 to 0.3125
- cotangent: bfloat16 [16, 2048, 768], P('dp', 'seq'), may hold values from -6 to 6
Outputs:
- input_grad: bfloat16 [16, 2048, 768], P('dp', 'seq')
- conv_grad: float32 [3, 768, 384], P(None, 'dp', 'seq')
The draws below stay inside these ranges and needn't reach their ends.
All inputs are finite; a program needn't handle non-finite values.
Results may differ from the reference program's by a relative error of at most 0.0054.
Values may be sent and summed in bfloat16 or wider, within the bound.
A program may use at most 64 MiB of HBM per device.

```python
import jax
import jax.numpy as jnp
from jax import lax

C = 768
F = 384
SAMP_DEV = 2
DILATION = 1024
SAMPLES = 16
LENGTH = 2048
N_DP = 8


def block_levels(key, dims, split, low, top_value):
    loudness = 1.0
    for position, parts in split:
        draws = jax.random.uniform(jax.random.fold_in(jax.random.fold_in(key, 6), position), (parts,), jnp.float32, low / len(split), top_value / len(split))
        loudness = loudness * jnp.repeat(jnp.exp(draws), dims[position] // parts).reshape((-1,) + (1,) * (len(dims) - 1 - position))
    return loudness


def noise(stream_key, extent, deviation, bound, pieces=(), kind=jnp.bfloat16):
    drawn = deviation * jax.random.normal(stream_key, extent, jnp.float32)
    if pieces:
        drawn = drawn * block_levels(stream_key, extent, pieces, -0.22, 0.18)
    return jnp.clip(drawn, -bound, bound).astype(kind)


def setup_inputs(seed: int = 0) -> dict:
    arg_keys = jax.random.split(jax.random.key(seed), 5)
    inputs = noise(arg_keys[0], (SAMPLES, LENGTH, C), 1.0, 6.0, ((0, 8), (1, 4)))
    conv_weight = noise(arg_keys[1], (3, C, F), (3 * C) ** -0.5, 0.125, ((1, 8), (2, 4)))
    point_weight = noise(arg_keys[2], (F, C), F ** -0.5, 0.3125, ((0, 4), (1, 8)))
    cotangent = noise(arg_keys[3], (SAMPLES, LENGTH, C), 1.0, 6.0, ((0, 8), (1, 4)))
    return dict(inputs=inputs, conv_weight=conv_weight, point_weight=point_weight, cotangent=cotangent)


EPSILON = 1e-06
GELU_SCALE = 0.7978845608028654
GELU_CUBIC = 0.044715

def gelu_tanh(values):
    return 0.5 * values * (1.0 + jnp.tanh(GELU_SCALE * (values + GELU_CUBIC * values * values * values)))

def gelu_slope(values):
    tangent = jnp.tanh(GELU_SCALE * (values + GELU_CUBIC * values * values * values))
    return 0.5 * (1.0 + tangent) + 0.5 * values * (1.0 - tangent * tangent) * GELU_SCALE * (1.0 + 3.0 * GELU_CUBIC * values * values)

def from_lower(array, distance):
    return jnp.concatenate([jnp.zeros_like(array[:, :distance]), array[:, :-distance]], axis=1)

def from_upper(array, distance):
    return jnp.concatenate([array[:, distance:], jnp.zeros_like(array[:, :distance])], axis=1)

def product(left, right):
    return jnp.dot(left, right, preferred_element_type=jnp.float32)

def outer_sum(left, right):
    return jnp.dot(left.astype(jnp.float32).T, right.astype(jnp.float32))

def reference(inputs, conv_weight, point_weight, cotangent):
    grad_scale = float(SAMPLES * LENGTH) ** (-0.5)
    row_count = SAMP_DEV * LENGTH

    def one_group(conv_sum, group):
        group_inputs, group_cot = group
        floats = group_inputs.astype(jnp.float32)
        row_scale = lax.rsqrt(lax.optimization_barrier(jnp.mean(floats * floats, axis=-1, keepdims=True)) + EPSILON)
        normed = floats * row_scale
        acted = gelu_tanh(normed).astype(jnp.bfloat16)
        acted_flat = acted.reshape(row_count, C)
        tap_low = product(acted_flat, conv_weight[0]).astype(jnp.bfloat16).reshape(SAMP_DEV, LENGTH, F)
        tap_high = product(acted_flat, conv_weight[2]).astype(jnp.bfloat16).reshape(SAMP_DEV, LENGTH, F)
        shifted_low = from_lower(tap_low, DILATION).reshape(row_count, F).astype(jnp.float32)
        shifted_high = from_upper(tap_high, DILATION).reshape(row_count, F).astype(jnp.float32)
        preact = shifted_low + product(acted_flat, conv_weight[1]) + shifted_high
        cot_flat = group_cot.reshape(row_count, C)
        grad_inner = product(cot_flat, point_weight.T)
        grad_pre = (grad_inner * gelu_slope(preact)).astype(jnp.bfloat16)
        grad_blocks = grad_pre.reshape(SAMP_DEV, LENGTH, F)
        grad_upper = from_upper(grad_blocks, DILATION).reshape(row_count, F)
        grad_lower = from_lower(grad_blocks, DILATION).reshape(row_count, F)
        grad_act = product(grad_upper, conv_weight[0].T) + product(grad_pre, conv_weight[1].T) + product(grad_lower, conv_weight[2].T)
        normed_flat = normed.reshape(row_count, C)
        scale_flat = row_scale.reshape(row_count, 1)
        grad_norm = grad_act * gelu_slope(normed_flat)
        center = lax.optimization_barrier(jnp.mean(grad_norm * normed_flat, axis=-1, keepdims=True))
        grad_input = cot_flat.astype(jnp.float32) + scale_flat * (grad_norm - normed_flat * center)
        conv_terms = jnp.stack([outer_sum(acted_flat, grad_upper), outer_sum(acted_flat, grad_pre), outer_sum(acted_flat, grad_lower)], axis=0) * grad_scale
        return (conv_sum + conv_terms, grad_input.astype(jnp.bfloat16).reshape(SAMP_DEV, LENGTH, C))
    groups = (inputs.reshape(N_DP, SAMP_DEV, LENGTH, C), cotangent.reshape(N_DP, SAMP_DEV, LENGTH, C))
    conv_grad, grad_groups = lax.scan(one_group, jnp.zeros((3, C, F), jnp.float32), groups)
    return (grad_groups.reshape(SAMPLES, LENGTH, C), conv_grad)
```

```python
import jax
import jax.numpy as jnp
from jax import lax
from jax.experimental import pallas as pl
from jax.experimental.pallas import tpu as pltpu
from jax.sharding import PartitionSpec as P

SPAN = 2


EPSILON = 1e-06
GELU_SCALE = 0.7978845608028654
GELU_CUBIC = 0.044715


def from_behind(x, axis, by):
    peers = lax.axis_size(axis)
    pairs = [(i, i + by) for i in range(peers) if 0 <= i + by < peers]
    return lax.ppermute(x, axis, pairs)


def gelu_tanh(values):
    return (
        0.5
        * values
        * (1.0 + jnp.tanh(GELU_SCALE * (values + GELU_CUBIC * values * values * values)))
    )


def gelu_slope(values):
    tangent = jnp.tanh(GELU_SCALE * (values + GELU_CUBIC * values * values * values))
    return 0.5 * (1.0 + tangent) + 0.5 * values * (1.0 - tangent * tangent) * GELU_SCALE * (
        1.0 + 3.0 * GELU_CUBIC * values * values
    )


def product(left, right):
    return jnp.dot(left, right, preferred_element_type=jnp.float32)


def outer_sum(left, right):
    return jnp.einsum("rc,rf->cf", left, right, preferred_element_type=jnp.float32)


def to_half(values):
    return lax.optimization_barrier(values.astype(jnp.bfloat16))


def from_lower(array):
    moved = from_behind(array, "seq", SPAN)
    return moved


def from_upper(array):
    moved = from_behind(array, "seq", -SPAN)
    return moved


def body(inputs, conv_weight, point_weight, cotangent):
    samp_count, bin_count, width = inputs.shape
    row_count = samp_count * bin_count
    grad_scale = float(row_count * lax.axis_size("dp") * lax.axis_size("seq")) ** (-0.5)
    columns = (
        lax.all_gather(conv_weight, "seq", axis=2, tiled=True),
        lax.all_gather(point_weight, "seq", axis=0, tiled=True),
    )
    conv_full, point_full = (
        lax.all_gather(columns[0], "dp", axis=1, tiled=True),
        lax.all_gather(columns[1], "dp", axis=1, tiled=True),
    )
    hidden = conv_full.shape[2]
    floats = inputs.astype(jnp.float32)
    row_scale = lax.rsqrt(jnp.mean(floats * floats, axis=-1, keepdims=True) + EPSILON)
    normed = floats * row_scale
    acted = gelu_tanh(normed).astype(jnp.bfloat16)
    acted_flat = acted.reshape(row_count, width)
    lower_acts = from_lower(acted).reshape(row_count, width)
    upper_acts = from_upper(acted).reshape(row_count, width)
    shifted_low = to_half(product(lower_acts, conv_full[0])).astype(jnp.float32)
    shifted_high = to_half(product(upper_acts, conv_full[2])).astype(jnp.float32)
    preact = shifted_low + product(acted_flat, conv_full[1]) + shifted_high
    cot_flat = cotangent.reshape(row_count, width)
    grad_inner = product(cot_flat, point_full.T)
    grad_pre = (grad_inner * gelu_slope(preact)).astype(jnp.bfloat16)
    grad_blocks = grad_pre.reshape(samp_count, bin_count, hidden)
    grad_upper = from_upper(grad_blocks).reshape(row_count, hidden)
    grad_lower = from_lower(grad_blocks).reshape(row_count, hidden)
    grad_act = (
        product(grad_upper, conv_full[0].T)
        + product(grad_pre, conv_full[1].T)
        + product(grad_lower, conv_full[2].T)
    )
    normed_flat = normed.reshape(row_count, width)
    scale_flat = row_scale.reshape(row_count, 1)
    grad_norm = grad_act * gelu_slope(normed_flat)
    center = jnp.mean(grad_norm * normed_flat, axis=-1, keepdims=True)
    grad_input = cot_flat.astype(jnp.float32) + scale_flat * (grad_norm - normed_flat * center)
    input_grad = grad_input.astype(jnp.bfloat16).reshape(samp_count, bin_count, width)
    conv_terms = (
        jnp.stack(
            [
                outer_sum(acted_flat, grad_upper),
                outer_sum(acted_flat, grad_pre),
                outer_sum(acted_flat, grad_lower),
            ],
            axis=0,
        )
        * grad_scale
    )
    partial_terms = lax.psum_scatter(conv_terms, "dp", scatter_dimension=1, tiled=True)
    conv_grad = lax.psum_scatter(partial_terms, "seq", scatter_dimension=2, tiled=True)
    return (input_grad, conv_grad)

MESH = pl.DeviceIdType.MESH
ZS, YS = 4, 2
ORDER = (1, 3, 2)


def fits(mesh):
    return mesh.shape["dp"] == ZS * YS and mesh.shape["seq"] == 2 * SPAN


def fused_kernel(
    grad_scale,
    x_ref, w_ref, cot_ref,
    out_ref, conv_ref,
    planes, w_halo, w_mid, w_point,
    acted, normed, slope, scale,
    mid, inner, tap_out, tap_in, pre_out, pre_in,
    g_halo, g_mid, own, sib_out, sib_in, y_out, y_in, z_out, z_in, last, x_out, x_in,
    z_s, z_r, yw_s, yw_r, xw_s, xw_r, dx_s, dx_r, dy_s, dy_r, sb_s, sb_r,
    tp_s, tp_r, gp_s, gp_r, cs_s, cs_r, cy_s, cy_r, cz_s, cz_r, cx_s, cx_r,
):
    rows, width = x_ref.shape
    hidden = mid.shape[1]
    part = w_ref.shape[0]
    half = part // 2
    lane = hidden // 4
    d = lax.axis_index("dp")
    s = lax.axis_index("seq")
    z, y = lax.div(d, YS), lax.rem(d, YS)
    x, c = lax.div(s, 2), lax.rem(s, 2)
    s_x = (1 - x) * 2 + c
    s_c = x * 2 + 1 - c
    d_y = z * YS + 1 - y
    sib, xn, yn = (d, s_c), (d, s_x), (d_y, s)

    def zdev(k):
        return (lax.rem(z + k, ZS) * YS + y, s)

    barrier = pltpu.get_barrier_semaphore()
    for dev in (sib, xn, yn, zdev(1), zdev(2), zdev(3)):
        pl.semaphore_signal(barrier, inc=1, device_id=dev, device_id_type=MESH)

    def remote(src, dst, ssem, rsem, dev):
        return pltpu.make_async_remote_copy(
            src_ref=src, dst_ref=dst, send_sem=ssem, recv_sem=rsem,
            device_id=dev, device_id_type=MESH)

    def piece(plane, dd, start=0, size=part):
        return planes.at[plane, pl.ds(pl.multiple_of(dd * part + start, 16), size), :]

    pending = []

    def send(src, dst, ssem, rsem, dev):
        copy = remote(src, dst, ssem, rsem, dev)
        copy.start()
        pending.append(copy)

    def arrived(ref, ssem, rsem, dev):
        remote(ref, ref, ssem, rsem, dev).wait_recv()

    def from_k(k, yy):
        return lax.rem(z + ZS - k, ZS) * YS + yy

    planes[s, pl.ds(pl.multiple_of(d * part, 16), part), :] = w_ref[...]
    pl.semaphore_wait(barrier, 6)

    def to_sib(plane, dd, n):
        ref = piece(plane, dd)
        send(ref, ref, sb_s.at[n], sb_r.at[n], sib)

    def spread(k):
        ref = piece(s, from_k(k, y))
        send(ref, ref, xw_s.at[k], xw_r.at[k], xn)
        send(ref, ref, yw_s.at[k], yw_r.at[k], yn)
        to_sib(s, from_k(k, y), k)

    for k in ORDER:
        ref = piece(s, d)
        send(ref, ref, z_s.at[k], z_r.at[k], zdev(k))
    spread(0)

    step = 32
    quarter = rows // 8

    def activations(q):
        def one(i, carry):
            at = pl.ds(pl.multiple_of(q * quarter + i * step, 16), step)
            v = x_ref[at, :].astype(jnp.float32)
            r = lax.rsqrt(jnp.mean(v * v, axis=-1, keepdims=True) + EPSILON)
            n = v * r
            n2 = n * n
            t = jnp.tanh(GELU_SCALE * (n + GELU_CUBIC * n2 * n))
            normed[at, :] = n
            acted[at, :] = (0.5 * n * (1.0 + t)).astype(jnp.bfloat16)
            slope[at, :] = 0.5 * (1.0 + t) + 0.5 * n * (1.0 - t * t) * GELU_SCALE * (
                1.0 + 3.0 * GELU_CUBIC * n2)
            scale[at, :] = jnp.broadcast_to(r, (step, 128))
            return carry
        lax.fori_loop(0, quarter // step, one, 0)

    def take_y(k):
        dd = from_k(k, 1 - y)
        arrived(piece(s, dd), yw_s.at[k], yw_r.at[k], yn)
        ref = piece(s, dd, 0, half)
        send(ref, ref, dx_s.at[k], dx_r.at[k], xn)
        to_sib(s, dd, 4 + k)

    def take_x(k):
        dd = from_k(k, y)
        arrived(piece(s_x, dd), xw_s.at[k], xw_r.at[k], xn)
        ref = piece(s_x, dd, half, half)
        send(ref, ref, dy_s.at[k], dy_r.at[k], yn)
        to_sib(s_x, dd, 8 + k)

    def take_diagonal(k):
        dd = from_k(k, 1 - y)
        arrived(piece(s_x, dd, 0, half), dx_s.at[k], dx_r.at[k], xn)
        arrived(piece(s_x, dd, half, half), dy_s.at[k], dy_r.at[k], yn)
        to_sib(s_x, dd, 12 + k)

    activations(0)
    activations(1)
    for n, k in enumerate(ORDER):
        arrived(piece(s, from_k(k, y)), z_s.at[k], z_r.at[k], zdev(k))
        spread(k)
        take_y(((0,) + ORDER)[n])
        take_x(((0,) + ORDER)[n])
        activations(2 + 2 * n)
        activations(3 + 2 * n)
    take_y(ORDER[2])
    take_x(ORDER[2])
    for k in (0,) + ORDER:
        take_diagonal(k)
    for plane, yy, n in ((s_c, y, 0), (s_c, 1 - y, 4), ((1 - x) * 2 + 1 - c, y, 8),
                         ((1 - x) * 2 + 1 - c, 1 - y, 12)):
        for k in range(ZS):
            arrived(piece(plane, from_k(k, yy)), sb_s.at[n + k], sb_r.at[n + k], sib)

    block = 128
    is_low = x == 0

    def assemble(i, carry):
        at = pl.ds(pl.multiple_of(i * block, 16), block)
        got = [planes[p, at, :] for p in range(4)]

        def columns(m):
            return jnp.concatenate([g[:, m * lane:(m + 1) * lane] for g in got], axis=1)

        w_halo[at, :] = jnp.where(is_low, columns(0), columns(2))
        w_mid[at, :] = columns(1)
        w_point[at, :] = columns(3)
        return carry

    lax.fori_loop(0, width // block, assemble, 0)

    chunks = 4
    size = rows // chunks

    def chunk(q):
        return pl.ds(q * size, size)

    for q in range(chunks):
        tap_out[chunk(q), :] = product(acted[chunk(q), :], w_halo[...]).astype(jnp.bfloat16)
        send(tap_out.at[chunk(q)], tap_in.at[chunk(q)], tp_s.at[q], tp_r.at[q], xn)

    for q in range(chunks):
        mid[chunk(q), :] = product(acted[chunk(q), :], w_mid[...])
        inner[chunk(q), :] = product(cot_ref[chunk(q), :], w_point[...])

    for q in range(chunks):
        arrived(tap_in.at[chunk(q)], tp_s.at[q], tp_r.at[q], xn)

        def one(i, carry):
            at = pl.ds(pl.multiple_of(q * size + i * step, 16), step)
            pre = mid[at, :] + tap_in[at, :].astype(jnp.float32)
            pre_out[at, :] = (inner[at, :] * gelu_slope(pre)).astype(jnp.bfloat16)
            return carry

        lax.fori_loop(0, size // step, one, 0)
        send(pre_out.at[chunk(q)], pre_in.at[chunk(q)], gp_s.at[q], gp_r.at[q], xn)

    over_rows = (((0,), (0,)), ((), ()))
    over_lanes = (((1,), (1,)), ((), ()))

    def outer(a, b):
        return lax.dot_general(a, b, over_rows, preferred_element_type=jnp.float32)

    def back(a, b):
        return lax.dot_general(a, b, over_lanes, preferred_element_type=jnp.float32)

    g_mid[...] = outer(acted[...], pre_out[...])

    for q in range(chunks):
        arrived(pre_in.at[chunk(q)], gp_s.at[q], gp_r.at[q], xn)
    g_halo[...] = outer(acted[...], pre_in[...])

    def pack(i, carry):
        at = pl.ds(pl.multiple_of(i * 64, 16), 64)
        a, b = g_halo[at, :] * grad_scale, g_mid[at, :] * grad_scale

        def columns(core):
            return jnp.concatenate(
                [g[:, p * lane:(p + 1) * lane] for g in (a, b) for p in (core, 2 + core)], axis=1)

        even, odd = columns(0), columns(1)
        first = c == 0
        own[at, :] = jnp.where(first, even, odd)
        sib_out[at, :] = jnp.where(first, odd, even).astype(jnp.bfloat16)
        return carry

    lax.fori_loop(0, width // 64, pack, 0)
    send(sib_out, sib_in, cs_s.at[0], cs_r.at[0], sib)

    def finish(q):
        act = back(pre_in[chunk(q), :], w_halo[...]) + back(pre_out[chunk(q), :], w_mid[...])
        mark = pl.ds(q * size, size)
        slope[mark, :] = act * slope[mark, :]

        def one(i, carry):
            at = pl.ds(pl.multiple_of(q * size + i * step, 16), step)
            g, n = slope[at, :], normed[at, :]
            center = jnp.mean(g * n, axis=-1, keepdims=True)
            r = scale[at, :][:, :1]
            out_ref[at, :] = (cot_ref[at, :].astype(jnp.float32) + r * (g - n * center)).astype(
                jnp.bfloat16)
            return carry

        lax.fori_loop(0, size // step, one, 0)

    def dest(k, yy):
        return pl.ds(pl.multiple_of((lax.rem(z + k, ZS) * YS + yy) * part, 16), part)

    arrived(sib_in, cs_s.at[0], cs_r.at[0], sib)
    for k in ORDER + (0,):
        at = dest(k, 1 - y)
        y_out[k] = (own[at, :] + sib_in[at, :].astype(jnp.float32)).astype(jnp.bfloat16)
        send(y_out.at[k], y_in.at[k], cy_s.at[k], cy_r.at[k], yn)
    finish(0)
    for n, k in enumerate(ORDER + (0,)):
        at = dest(k, y)
        arrived(y_in.at[k], cy_s.at[k], cy_r.at[k], yn)
        total = own[at, :] + sib_in[at, :].astype(jnp.float32) + y_in[k].astype(jnp.float32)
        if k:
            z_out[k] = total.astype(jnp.bfloat16)
            send(z_out.at[k], z_in.at[k], cz_s.at[k], cz_r.at[k], zdev(k))
        else:
            last[...] = total
    finish(1)
    finish(2)
    for k in ORDER:
        arrived(z_in.at[k], cz_s.at[k], cz_r.at[k], zdev(k))
    last[...] = last[...] + (z_in[1].astype(jnp.float32) + z_in[2].astype(jnp.float32)
                             + z_in[3].astype(jnp.float32))
    x_out[...] = last[...].astype(jnp.bfloat16)
    send(x_out, x_in, cx_s.at[0], cx_r.at[0], xn)
    finish(3)
    arrived(x_in, cx_s.at[0], cx_r.at[0], xn)
    mine, theirs = last[...], x_in[...].astype(jnp.float32)

    def pick(v, slot):
        low = v[:, (2 * slot) * lane:(2 * slot + 1) * lane]
        high = v[:, (2 * slot + 1) * lane:(2 * slot + 2) * lane]
        return jnp.where(is_low, low, high)

    own_halo, their_halo = pick(mine, 0), pick(theirs, 0)
    conv_ref[0] = jnp.where(is_low, own_halo, their_halo)
    conv_ref[1] = pick(mine, 1) + pick(theirs, 1)
    conv_ref[2] = jnp.where(is_low, their_halo, own_halo)
    for copy in pending:
        copy.wait_send()


def fused_body(inputs, conv_weight, point_weight, cotangent):
    samp_count, bin_count, width = inputs.shape
    rows = samp_count * bin_count
    part = conv_weight.shape[1]
    hidden = conv_weight.shape[2] * lax.axis_size("seq")
    grad_scale = float(rows * lax.axis_size("dp") * lax.axis_size("seq")) ** (-0.5)
    packed = jnp.concatenate([conv_weight[0], conv_weight[1], conv_weight[2], point_weight.T], axis=1)
    bf, f32 = jnp.bfloat16, jnp.float32

    def vmem(kind, *dims):
        return pltpu.VMEM(dims, kind)

    def sems(n):
        return [pltpu.SemaphoreType.DMA((n,))] * 2

    whole = pl.BlockSpec(memory_space=pltpu.VMEM)
    grad, conv_grad = pl.pallas_call(
        lambda *refs: fused_kernel(grad_scale, *refs),
        out_shape=(
            jax.ShapeDtypeStruct((rows, width), bf),
            jax.ShapeDtypeStruct(conv_weight.shape, f32),
        ),
        in_specs=[whole] * 3,
        out_specs=(whole, whole),
        scratch_shapes=[
            vmem(bf, 4, width, hidden), vmem(bf, width, hidden), vmem(bf, width, hidden),
            vmem(bf, width, hidden),
            vmem(bf, rows, width), vmem(f32, rows, width), vmem(f32, rows, width),
            vmem(f32, rows, 128),
            vmem(f32, rows, hidden), vmem(f32, rows, hidden), vmem(bf, rows, hidden),
            vmem(bf, rows, hidden), vmem(bf, rows, hidden), vmem(bf, rows, hidden),
            vmem(f32, width, hidden), vmem(f32, width, hidden), vmem(f32, width, hidden),
            vmem(bf, width, hidden), vmem(bf, width, hidden),
            vmem(bf, 4, part, hidden), vmem(bf, 4, part, hidden),
            vmem(bf, 4, part, hidden), vmem(bf, 4, part, hidden),
            vmem(f32, part, hidden), vmem(bf, part, hidden), vmem(bf, part, hidden),
            *sems(4), *sems(4), *sems(4), *sems(4), *sems(4), *sems(16),
            *sems(4), *sems(4), *sems(1), *sems(4), *sems(4), *sems(1),
        ],
        compiler_params=pltpu.CompilerParams(
            collective_id=0, has_side_effects=True, vmem_limit_bytes=56 * 1024 * 1024),
    )(inputs.reshape(rows, width), packed, cotangent.reshape(rows, width))
    return grad.reshape(samp_count, bin_count, width), conv_grad


def solution(mesh):
    return jax.shard_map(
        fused_body if fits(mesh) else body,
        mesh=mesh,
        in_specs=(P("dp", "seq", None), P(None, "dp", "seq"), P("seq", "dp"), P("dp", "seq", None)),
        out_specs=(P("dp", "seq", None), P(None, "dp", "seq")),
        check_vma=False,
    )
```

```python
import jax
import jax.numpy as jnp
from jax import lax
from jax.experimental import pallas as pl
from jax.experimental.pallas import tpu as pltpu
from jax.sharding import PartitionSpec as P

SPAN = 2


EPSILON = 1e-06
GELU_SCALE = 0.7978845608028654
GELU_CUBIC = 0.044715


def from_behind(x, axis, by):
    peers = lax.axis_size(axis)
    pairs = [(i, i + by) for i in range(peers) if 0 <= i + by < peers]
    return lax.ppermute(x, axis, pairs)


def gelu_tanh(values):
    return (
        0.5
        * values
        * (1.0 + jnp.tanh(GELU_SCALE * (values + GELU_CUBIC * values * values * values)))
    )


def gelu_slope(values):
    tangent = jnp.tanh(GELU_SCALE * (values + GELU_CUBIC * values * values * values))
    return 0.5 * (1.0 + tangent) + 0.5 * values * (1.0 - tangent * tangent) * GELU_SCALE * (
        1.0 + 3.0 * GELU_CUBIC * values * values
    )


def product(left, right):
    return jnp.dot(left, right, preferred_element_type=jnp.float32)


def outer_sum(left, right):
    return jnp.einsum("rc,rf->cf", left, right, preferred_element_type=jnp.float32)


def to_half(values):
    return lax.optimization_barrier(values.astype(jnp.bfloat16))


def from_lower(array):
    moved = from_behind(array, "seq", SPAN)
    return moved


def from_upper(array):
    moved = from_behind(array, "seq", -SPAN)
    return moved


def body(inputs, conv_weight, point_weight, cotangent):
    samp_count, bin_count, width = inputs.shape
    row_count = samp_count * bin_count
    grad_scale = float(row_count * lax.axis_size("dp") * lax.axis_size("seq")) ** (-0.5)
    columns = (
        lax.all_gather(conv_weight, "seq", axis=2, tiled=True),
        lax.all_gather(point_weight, "seq", axis=0, tiled=True),
    )
    conv_full, point_full = (
        lax.all_gather(columns[0], "dp", axis=1, tiled=True),
        lax.all_gather(columns[1], "dp", axis=1, tiled=True),
    )
    hidden = conv_full.shape[2]
    floats = inputs.astype(jnp.float32)
    row_scale = lax.rsqrt(jnp.mean(floats * floats, axis=-1, keepdims=True) + EPSILON)
    normed = floats * row_scale
    acted = gelu_tanh(normed).astype(jnp.bfloat16)
    acted_flat = acted.reshape(row_count, width)
    lower_acts = from_lower(acted).reshape(row_count, width)
    upper_acts = from_upper(acted).reshape(row_count, width)
    shifted_low = to_half(product(lower_acts, conv_full[0])).astype(jnp.float32)
    shifted_high = to_half(product(upper_acts, conv_full[2])).astype(jnp.float32)
    preact = shifted_low + product(acted_flat, conv_full[1]) + shifted_high
    cot_flat = cotangent.reshape(row_count, width)
    grad_inner = product(cot_flat, point_full.T)
    grad_pre = (grad_inner * gelu_slope(preact)).astype(jnp.bfloat16)
    grad_blocks = grad_pre.reshape(samp_count, bin_count, hidden)
    grad_upper = from_upper(grad_blocks).reshape(row_count, hidden)
    grad_lower = from_lower(grad_blocks).reshape(row_count, hidden)
    grad_act = (
        product(grad_upper, conv_full[0].T)
        + product(grad_pre, conv_full[1].T)
        + product(grad_lower, conv_full[2].T)
    )
    normed_flat = normed.reshape(row_count, width)
    scale_flat = row_scale.reshape(row_count, 1)
    grad_norm = grad_act * gelu_slope(normed_flat)
    center = jnp.mean(grad_norm * normed_flat, axis=-1, keepdims=True)
    grad_input = cot_flat.astype(jnp.float32) + scale_flat * (grad_norm - normed_flat * center)
    input_grad = grad_input.astype(jnp.bfloat16).reshape(samp_count, bin_count, width)
    conv_terms = (
        jnp.stack(
            [
                outer_sum(acted_flat, grad_upper),
                outer_sum(acted_flat, grad_pre),
                outer_sum(acted_flat, grad_lower),
            ],
            axis=0,
        )
        * grad_scale
    )
    partial_terms = lax.psum_scatter(conv_terms, "dp", scatter_dimension=1, tiled=True)
    conv_grad = lax.psum_scatter(partial_terms, "seq", scatter_dimension=2, tiled=True)
    return (input_grad, conv_grad)

MESH = pl.DeviceIdType.MESH
ZS, YS = 4, 2
ORDER = (1, 3, 2)


def fits(mesh):
    return mesh.shape["dp"] == ZS * YS and mesh.shape["seq"] == 2 * SPAN


def fused_kernel(
    grad_scale,
    x_ref, conv_w_ref, point_w_ref, cot_ref,
    out_ref, conv_ref,
    w_own, w_in, first_w, rest_w, w_halo, w_mid, w_point,
    acted, normed, slope, scale,
    mid, inner, tap_out, tap_in, pre_out, pre_in,
    grads, own, sib_out, sib_in, y_out, y_in, z_out, z_in, last, x_out, x_in,
    wx_s, wx_r, wz_s, wz_r, wy_s, wy_r, wc_s, wc_r,
    tp_s, tp_r, gp_s, gp_r, cs_s, cs_r, cy_s, cy_r, cz_s, cz_r, cx_s, cx_r,
):
    rows, width = x_ref.shape
    hidden = mid.shape[1]
    part = w_own.shape[0]
    lane = hidden // 4
    d = lax.axis_index("dp")
    s = lax.axis_index("seq")
    z, y = lax.div(d, YS), lax.rem(d, YS)
    x, c = lax.div(s, 2), lax.rem(s, 2)
    is_low = x == 0
    sib = (d, x * 2 + 1 - c)
    xn = (d, (1 - x) * 2 + c)
    yn = (z * YS + 1 - y, s)

    def zdev(k):
        return (lax.rem(z + k, ZS) * YS + y, s)

    barrier = pltpu.get_barrier_semaphore()
    for dev in (sib, xn, yn, zdev(1), zdev(2), zdev(3)):
        pl.semaphore_signal(barrier, inc=1, device_id=dev, device_id_type=MESH)

    def remote(src, dst, ssem, rsem, dev):
        return pltpu.make_async_remote_copy(
            src_ref=src, dst_ref=dst, send_sem=ssem, recv_sem=rsem,
            device_id=dev, device_id_type=MESH)

    pending = []

    def send(src, dst, ssem, rsem, dev):
        copy = remote(src, dst, ssem, rsem, dev)
        copy.start()
        pending.append(copy)

    def arrived(ref, ssem, rsem, dev):
        remote(ref, ref, ssem, rsem, dev).wait_recv()

    def from_k(k, yy):
        return lax.rem(z + ZS - k, ZS) * YS + yy

    step = 32
    eighth = rows // 8

    def activations(q):
        def one(i, carry):
            at = pl.ds(pl.multiple_of(q * eighth + i * step, 16), step)
            v = x_ref[at, :].astype(jnp.float32)
            r = lax.rsqrt(jnp.mean(v * v, axis=-1, keepdims=True) + EPSILON)
            n = v * r
            n2 = n * n
            t = jnp.tanh(GELU_SCALE * (n + GELU_CUBIC * n2 * n))
            normed[at, :] = n
            acted[at, :] = (0.5 * n * (1.0 + t)).astype(jnp.bfloat16)
            slope[at, :] = 0.5 * (1.0 + t) + 0.5 * n * (1.0 - t * t) * GELU_SCALE * (
                1.0 + 3.0 * GELU_CUBIC * n2)
            scale[at, :] = jnp.broadcast_to(r, (step, 128))
            return carry
        lax.fori_loop(0, eighth // step, one, 0)

    w_own[...] = jnp.concatenate(
        [conv_w_ref[0], conv_w_ref[2], conv_w_ref[1],
         point_w_ref[...].astype(jnp.float32).T.astype(jnp.bfloat16)], axis=1)
    pl.semaphore_wait(barrier, 6)
    send(w_own, w_in, wx_s.at[0], wx_r.at[0], xn)
    activations(0)
    activations(1)
    arrived(w_in, wx_s.at[0], wx_r.at[0], xn)

    mine, theirs = w_own[...], w_in[...]
    low, high = jnp.where(is_low, mine, theirs), jnp.where(is_low, theirs, mine)

    def live(v):
        return jnp.where(is_low, v[:, :lane], v[:, lane:2 * lane])

    at_own = pl.ds(pl.multiple_of(d * part, 16), part)
    first_w[c, at_own, :] = jnp.concatenate(
        [live(low), live(high), jnp.zeros((part, 256 - 2 * lane), jnp.bfloat16)], axis=1)
    rest_w[c, at_own, :] = jnp.concatenate([low[:, 2 * lane:], high[:, 2 * lane:]], axis=1)

    bufs = (first_w, rest_w)

    def piece(p, core, dd):
        return bufs[p].at[core, pl.ds(pl.multiple_of(dd * part, 16), part), :]

    def forward(p, k):
        ref = piece(p, c, from_k(k, y))
        send(ref, ref, wy_s.at[p, k], wy_r.at[p, k], yn)
        send(ref, ref, wc_s.at[p, k], wc_r.at[p, k], sib)

    def begin(p):
        ref = piece(p, c, d)
        for k in ORDER:
            send(ref, ref, wz_s.at[p, k], wz_r.at[p, k], zdev(k))
        forward(p, 0)

    def take_z(p, k):
        arrived(piece(p, c, from_k(k, y)), wz_s.at[p, k], wz_r.at[p, k], zdev(k))
        forward(p, k)

    def take_y(p, k):
        ref = piece(p, c, from_k(k, 1 - y))
        arrived(ref, wy_s.at[p, k], wy_r.at[p, k], yn)
        send(ref, ref, wc_s.at[p, 4 + k], wc_r.at[p, 4 + k], sib)

    def take_core(p):
        for n, yy in ((0, y), (4, 1 - y)):
            for k in range(ZS):
                arrived(piece(p, 1 - c, from_k(k, yy)), wc_s.at[p, n + k], wc_r.at[p, n + k], sib)

    begin(0)
    activations(2)
    for n, k in enumerate(ORDER):
        take_z(0, k)
        activations(3 + n)
    begin(1)
    for n, k in enumerate((0,) + ORDER):
        take_y(0, k)
        if n < 2:
            activations(6 + n)
    take_core(0)

    block = 128

    def assemble_first(i, carry):
        at = pl.ds(pl.multiple_of(i * block, 16), block)
        even, odd = first_w[0, at, :], first_w[1, at, :]
        w_halo[at, :] = jnp.concatenate(
            [even[:, :lane], odd[:, :lane], even[:, lane:2 * lane], odd[:, lane:2 * lane]], axis=1)
        return carry

    lax.fori_loop(0, width // block, assemble_first, 0)

    chunks = 4
    size = rows // chunks

    def chunk(q):
        return pl.ds(q * size, size)

    def tap(q):
        tap_out[chunk(q), :] = product(acted[chunk(q), :], w_halo[...]).astype(jnp.bfloat16)
        send(tap_out.at[chunk(q)], tap_in.at[chunk(q)], tp_s.at[q], tp_r.at[q], xn)

    tap(0)
    for k in ORDER:
        take_z(1, k)
    for q in range(1, chunks):
        tap(q)
    for k in (0,) + ORDER:
        take_y(1, k)
    take_core(1)

    def assemble_rest(i, carry):
        at = pl.ds(pl.multiple_of(i * block, 16), block)
        even, odd = rest_w[0, at, :], rest_w[1, at, :]

        def columns(m):
            return jnp.concatenate(
                [v[:, p * lane:(p + 1) * lane] for p in (m, 2 + m) for v in (even, odd)], axis=1)

        w_mid[at, :] = columns(0)
        w_point[at, :] = columns(1)
        return carry

    lax.fori_loop(0, width // block, assemble_rest, 0)

    for q in range(chunks):
        mid[chunk(q), :] = product(acted[chunk(q), :], w_mid[...])
        inner[chunk(q), :] = product(cot_ref[chunk(q), :], w_point[...])

    for q in range(chunks):
        arrived(tap_in.at[chunk(q)], tp_s.at[q], tp_r.at[q], xn)

        def one(i, carry):
            at = pl.ds(pl.multiple_of(q * size + i * step, 16), step)
            pre = mid[at, :] + tap_in[at, :].astype(jnp.float32)
            pre_out[at, :] = (inner[at, :] * gelu_slope(pre)).astype(jnp.bfloat16)
            return carry

        lax.fori_loop(0, size // step, one, 0)
        send(pre_out.at[chunk(q)], pre_in.at[chunk(q)], gp_s.at[q], gp_r.at[q], xn)

    over_rows = (((0,), (0,)), ((), ()))
    over_lanes = (((1,), (1,)), ((), ()))

    def outer(a, b):
        return lax.dot_general(a, b, over_rows, preferred_element_type=jnp.float32)

    def back(a, b):
        return lax.dot_general(a, b, over_lanes, preferred_element_type=jnp.float32)

    def share_core(t):
        def pack(i, carry):
            at = pl.ds(pl.multiple_of(i * 64, 16), 64)
            g = grads[t, at, :] * grad_scale
            blank = jnp.zeros((64, 256 - 2 * lane), jnp.float32)

            def columns(core):
                return jnp.concatenate(
                    [g[:, p * lane:(p + 1) * lane] for p in (core, 2 + core)] + [blank], axis=1)

            even, odd = columns(0), columns(1)
            own[t, at, :] = jnp.where(c == 0, even, odd)
            sib_out[t, at, :] = jnp.where(c == 0, odd, even).astype(jnp.bfloat16)
            return carry

        lax.fori_loop(0, width // 64, pack, 0)
        send(sib_out.at[t], sib_in.at[t], cs_s.at[t], cs_r.at[t], sib)

    def dest(k, yy):
        return pl.ds(pl.multiple_of((lax.rem(z + k, ZS) * YS + yy) * part, 16), part)

    def share_y(t):
        arrived(sib_in.at[t], cs_s.at[t], cs_r.at[t], sib)
        for k in ORDER + (0,):
            at = dest(k, 1 - y)
            y_out[t, k] = (own[t, at, :] + sib_in[t, at, :].astype(jnp.float32)).astype(jnp.bfloat16)
            send(y_out.at[t, k], y_in.at[t, k], cy_s.at[t, k], cy_r.at[t, k], yn)

    def share_z(t):
        for k in ORDER + (0,):
            at = dest(k, y)
            arrived(y_in.at[t, k], cy_s.at[t, k], cy_r.at[t, k], yn)
            total = (own[t, at, :] + sib_in[t, at, :].astype(jnp.float32)
                     + y_in[t, k].astype(jnp.float32))
            if k:
                z_out[t, k] = total.astype(jnp.bfloat16)
                send(z_out.at[t, k], z_in.at[t, k], cz_s.at[t, k], cz_r.at[t, k], zdev(k))
            else:
                last[t] = total

    def share_x(t):
        for k in ORDER:
            arrived(z_in.at[t, k], cz_s.at[t, k], cz_r.at[t, k], zdev(k))
        total = last[t] + (z_in[t, 1].astype(jnp.float32) + z_in[t, 2].astype(jnp.float32)
                           + z_in[t, 3].astype(jnp.float32))
        last[t] = total
        x_out[t] = total.astype(jnp.bfloat16)
        send(x_out.at[t], x_in.at[t], cx_s.at[t], cx_r.at[t], xn)

    def finish(q):
        act = back(pre_in[chunk(q), :], w_halo[...]) + back(pre_out[chunk(q), :], w_mid[...])
        slope[chunk(q), :] = act * slope[chunk(q), :]

        def one(i, carry):
            at = pl.ds(pl.multiple_of(q * size + i * step, 16), step)
            g, n = slope[at, :], normed[at, :]
            center = jnp.mean(g * n, axis=-1, keepdims=True)
            r = scale[at, :][:, :1]
            out_ref[at, :] = (cot_ref[at, :].astype(jnp.float32) + r * (g - n * center)).astype(
                jnp.bfloat16)
            return carry

        lax.fori_loop(0, size // step, one, 0)

    def halo_term(q):
        arrived(pre_in.at[chunk(q)], gp_s.at[q], gp_r.at[q], xn)
        term = outer(acted[chunk(q), :], pre_in[chunk(q), :])
        grads[0] = term if q == 0 else grads[0] + term

    grads[1] = outer(acted[...], pre_out[...])
    share_core(1)
    share_y(1)
    halo_term(0)
    share_z(1)
    finish(0)
    halo_term(1)
    share_x(1)
    finish(1)
    halo_term(2)
    halo_term(3)
    share_core(0)
    share_y(0)
    share_z(0)
    finish(2)
    share_x(0)
    finish(3)

    def pick(v):
        return jnp.where(is_low, v[:, :lane], v[:, lane:2 * lane])

    arrived(x_in.at[1], cx_s.at[1], cx_r.at[1], xn)
    conv_ref[1] = pick(last[1]) + pick(x_in[1].astype(jnp.float32))
    arrived(x_in.at[0], cx_s.at[0], cx_r.at[0], xn)
    own_halo, their_halo = pick(last[0]), pick(x_in[0].astype(jnp.float32))
    conv_ref[0] = jnp.where(is_low, own_halo, their_halo)
    conv_ref[2] = jnp.where(is_low, their_halo, own_halo)
    for copy in pending:
        copy.wait_send()


def fused_body(inputs, conv_weight, point_weight, cotangent):
    samp_count, bin_count, width = inputs.shape
    rows = samp_count * bin_count
    part = conv_weight.shape[1]
    hidden = conv_weight.shape[2] * lax.axis_size("seq")
    grad_scale = float(rows * lax.axis_size("dp") * lax.axis_size("seq")) ** (-0.5)
    bf, f32 = jnp.bfloat16, jnp.float32

    def vmem(kind, *dims):
        return pltpu.VMEM(dims, kind)

    def sems(*n):
        return [pltpu.SemaphoreType.DMA(n)] * 2

    whole = pl.BlockSpec(memory_space=pltpu.VMEM)
    grad, conv_grad = pl.pallas_call(
        lambda *refs: fused_kernel(grad_scale, *refs),
        out_shape=(
            jax.ShapeDtypeStruct((rows, width), bf),
            jax.ShapeDtypeStruct(conv_weight.shape, f32),
        ),
        in_specs=[whole] * 4,
        out_specs=(whole, whole),
        scratch_shapes=[
            vmem(bf, part, hidden), vmem(bf, part, hidden),
            vmem(bf, 2, width, 256), vmem(bf, 2, width, hidden),
            vmem(bf, width, hidden), vmem(bf, width, hidden), vmem(bf, width, hidden),
            vmem(bf, rows, width), vmem(f32, rows, width), vmem(f32, rows, width),
            vmem(f32, rows, 128),
            vmem(f32, rows, hidden), vmem(f32, rows, hidden), vmem(bf, rows, hidden),
            vmem(bf, rows, hidden), vmem(bf, rows, hidden), vmem(bf, rows, hidden),
            vmem(f32, 2, width, hidden), vmem(f32, 2, width, 256),
            vmem(bf, 2, width, 256), vmem(bf, 2, width, 256),
            vmem(bf, 2, 4, part, 256), vmem(bf, 2, 4, part, 256),
            vmem(bf, 2, 4, part, 256), vmem(bf, 2, 4, part, 256),
            vmem(f32, 2, part, 256), vmem(bf, 2, part, 256), vmem(bf, 2, part, 256),
            *sems(1), *sems(2, 4), *sems(2, 4), *sems(2, 8),
            *sems(4), *sems(4), *sems(2), *sems(2, 4), *sems(2, 4), *sems(2),
        ],
        compiler_params=pltpu.CompilerParams(
            collective_id=0, has_side_effects=True, vmem_limit_bytes=56 * 1024 * 1024),
    )(inputs.reshape(rows, width), conv_weight, point_weight, cotangent.reshape(rows, width))
    return grad.reshape(samp_count, bin_count, width), conv_grad


def solution(mesh):
    return jax.shard_map(
        fused_body if fits(mesh) else body,
        mesh=mesh,
        in_specs=(P("dp", "seq", None), P(None, "dp", "seq"), P("seq", "dp"), P("dp", "seq", None)),
        out_specs=(P("dp", "seq", None), P(None, "dp", "seq")),
        check_vma=False,
    )
```

```python
import jax
import jax.numpy as jnp
from jax import lax
from jax.experimental import pallas as pl
from jax.experimental.pallas import tpu as pltpu
from jax.sharding import PartitionSpec as P

SPAN = 2


EPSILON = 1e-06
GELU_SCALE = 0.7978845608028654
GELU_CUBIC = 0.044715


def from_behind(x, axis, by):
    peers = lax.axis_size(axis)
    pairs = [(i, i + by) for i in range(peers) if 0 <= i + by < peers]
    return lax.ppermute(x, axis, pairs)


def gelu_tanh(values):
    return (
        0.5
        * values
        * (1.0 + jnp.tanh(GELU_SCALE * (values + GELU_CUBIC * values * values * values)))
    )


def gelu_slope(values):
    tangent = jnp.tanh(GELU_SCALE * (values + GELU_CUBIC * values * values * values))
    return 0.5 * (1.0 + tangent) + 0.5 * values * (1.0 - tangent * tangent) * GELU_SCALE * (
        1.0 + 3.0 * GELU_CUBIC * values * values
    )


def product(left, right):
    return jnp.dot(left, right, preferred_element_type=jnp.float32)


def outer_sum(left, right):
    return jnp.einsum("rc,rf->cf", left, right, preferred_element_type=jnp.float32)


def to_half(values):
    return lax.optimization_barrier(values.astype(jnp.bfloat16))


def from_lower(array):
    moved = from_behind(array, "seq", SPAN)
    return moved


def from_upper(array):
    moved = from_behind(array, "seq", -SPAN)
    return moved


def body(inputs, conv_weight, point_weight, cotangent):
    samp_count, bin_count, width = inputs.shape
    row_count = samp_count * bin_count
    grad_scale = float(row_count * lax.axis_size("dp") * lax.axis_size("seq")) ** (-0.5)
    columns = (
        lax.all_gather(conv_weight, "seq", axis=2, tiled=True),
        lax.all_gather(point_weight, "seq", axis=0, tiled=True),
    )
    conv_full, point_full = (
        lax.all_gather(columns[0], "dp", axis=1, tiled=True),
        lax.all_gather(columns[1], "dp", axis=1, tiled=True),
    )
    hidden = conv_full.shape[2]
    floats = inputs.astype(jnp.float32)
    row_scale = lax.rsqrt(jnp.mean(floats * floats, axis=-1, keepdims=True) + EPSILON)
    normed = floats * row_scale
    acted = gelu_tanh(normed).astype(jnp.bfloat16)
    acted_flat = acted.reshape(row_count, width)
    lower_acts = from_lower(acted).reshape(row_count, width)
    upper_acts = from_upper(acted).reshape(row_count, width)
    shifted_low = to_half(product(lower_acts, conv_full[0])).astype(jnp.float32)
    shifted_high = to_half(product(upper_acts, conv_full[2])).astype(jnp.float32)
    preact = shifted_low + product(acted_flat, conv_full[1]) + shifted_high
    cot_flat = cotangent.reshape(row_count, width)
    grad_inner = product(cot_flat, point_full.T)
    grad_pre = (grad_inner * gelu_slope(preact)).astype(jnp.bfloat16)
    grad_blocks = grad_pre.reshape(samp_count, bin_count, hidden)
    grad_upper = from_upper(grad_blocks).reshape(row_count, hidden)
    grad_lower = from_lower(grad_blocks).reshape(row_count, hidden)
    grad_act = (
        product(grad_upper, conv_full[0].T)
        + product(grad_pre, conv_full[1].T)
        + product(grad_lower, conv_full[2].T)
    )
    normed_flat = normed.reshape(row_count, width)
    scale_flat = row_scale.reshape(row_count, 1)
    grad_norm = grad_act * gelu_slope(normed_flat)
    center = jnp.mean(grad_norm * normed_flat, axis=-1, keepdims=True)
    grad_input = cot_flat.astype(jnp.float32) + scale_flat * (grad_norm - normed_flat * center)
    input_grad = grad_input.astype(jnp.bfloat16).reshape(samp_count, bin_count, width)
    conv_terms = (
        jnp.stack(
            [
                outer_sum(acted_flat, grad_upper),
                outer_sum(acted_flat, grad_pre),
                outer_sum(acted_flat, grad_lower),
            ],
            axis=0,
        )
        * grad_scale
    )
    partial_terms = lax.psum_scatter(conv_terms, "dp", scatter_dimension=1, tiled=True)
    conv_grad = lax.psum_scatter(partial_terms, "seq", scatter_dimension=2, tiled=True)
    return (input_grad, conv_grad)

MESH = pl.DeviceIdType.MESH
ZS, YS = 4, 2
ORDER = (1, 3, 2)


def fits(mesh):
    return mesh.shape["dp"] == ZS * YS and mesh.shape["seq"] == 2 * SPAN


def fused_kernel(
    grad_scale,
    x_hbm, conv_w_ref, point_w_ref, cot_hbm,
    out_hbm, conv_ref,
    x_ref, cot_ref, out_ref, io_s,
    w_own, w_in, first_w, rest_w, w_halo, w_mid, w_point,
    acted, normed, slope, scale,
    mid, inner, tap_out, tap_in, pre_out, pre_in,
    grads, own, sib_out, sib_in, y_out, y_in, z_out, z_in, last, x_out, x_in,
    wx_s, wx_r, wz_s, wz_r, wy_s, wy_r, wc_s, wc_r,
    tp_s, tp_r, gp_s, gp_r, cs_s, cs_r, cy_s, cy_r, cz_s, cz_r, cx_s, cx_r,
):
    rows, width = x_ref.shape
    hidden = mid.shape[1]
    part = w_own.shape[0]
    lane = hidden // 4
    d = lax.axis_index("dp")
    s = lax.axis_index("seq")
    z, y = lax.div(d, YS), lax.rem(d, YS)
    x, c = lax.div(s, 2), lax.rem(s, 2)
    is_low = x == 0
    sib = (d, x * 2 + 1 - c)
    xn = (d, (1 - x) * 2 + c)
    yn = (z * YS + 1 - y, s)

    def zdev(k):
        return (lax.rem(z + k, ZS) * YS + y, s)

    load_x = pltpu.make_async_copy(x_hbm, x_ref, io_s.at[0])
    load_cot = pltpu.make_async_copy(cot_hbm, cot_ref, io_s.at[1])
    load_x.start()
    load_cot.start()
    barrier = pltpu.get_barrier_semaphore()
    for dev in (sib, xn, yn, zdev(1), zdev(2), zdev(3)):
        pl.semaphore_signal(barrier, inc=1, device_id=dev, device_id_type=MESH)

    def remote(src, dst, ssem, rsem, dev):
        return pltpu.make_async_remote_copy(
            src_ref=src, dst_ref=dst, send_sem=ssem, recv_sem=rsem,
            device_id=dev, device_id_type=MESH)

    pending = []

    def send(src, dst, ssem, rsem, dev):
        copy = remote(src, dst, ssem, rsem, dev)
        copy.start()
        pending.append(copy)

    def arrived(ref, ssem, rsem, dev):
        remote(ref, ref, ssem, rsem, dev).wait_recv()

    def from_k(k, yy):
        return lax.rem(z + ZS - k, ZS) * YS + yy

    step = 32
    eighth = rows // 8

    def activations(q):
        def one(i, carry):
            at = pl.ds(pl.multiple_of(q * eighth + i * step, 16), step)
            v = x_ref[at, :].astype(jnp.float32)
            r = lax.rsqrt(jnp.mean(v * v, axis=-1, keepdims=True) + EPSILON)
            n = v * r
            n2 = n * n
            t = jnp.tanh(GELU_SCALE * (n + GELU_CUBIC * n2 * n))
            normed[at, :] = n
            acted[at, :] = (0.5 * n * (1.0 + t)).astype(jnp.bfloat16)
            slope[at, :] = 0.5 * (1.0 + t) + 0.5 * n * (1.0 - t * t) * GELU_SCALE * (
                1.0 + 3.0 * GELU_CUBIC * n2)
            scale[at, :] = jnp.broadcast_to(r, (step, 128))
            return carry
        lax.fori_loop(0, eighth // step, one, 0)

    w_own[...] = jnp.concatenate(
        [conv_w_ref[0], conv_w_ref[2], conv_w_ref[1],
         point_w_ref[...].astype(jnp.float32).T.astype(jnp.bfloat16)], axis=1)
    pl.semaphore_wait(barrier, 6)
    send(w_own, w_in, wx_s.at[0], wx_r.at[0], xn)
    load_x.wait()
    activations(0)
    activations(1)
    arrived(w_in, wx_s.at[0], wx_r.at[0], xn)

    mine, theirs = w_own[...], w_in[...]
    low, high = jnp.where(is_low, mine, theirs), jnp.where(is_low, theirs, mine)

    def live(v):
        return jnp.where(is_low, v[:, :lane], v[:, lane:2 * lane])

    at_own = pl.ds(pl.multiple_of(d * part, 16), part)
    first_w[c, at_own, :] = jnp.concatenate(
        [live(low), live(high), jnp.zeros((part, 256 - 2 * lane), jnp.bfloat16)], axis=1)
    rest_w[c, at_own, :] = jnp.concatenate([low[:, 2 * lane:], high[:, 2 * lane:]], axis=1)

    bufs = (first_w, rest_w)

    def piece(p, core, dd):
        return bufs[p].at[core, pl.ds(pl.multiple_of(dd * part, 16), part), :]

    def forward(p, k):
        ref = piece(p, c, from_k(k, y))
        send(ref, ref, wy_s.at[p, k], wy_r.at[p, k], yn)
        send(ref, ref, wc_s.at[p, k], wc_r.at[p, k], sib)

    def begin(p):
        ref = piece(p, c, d)
        for k in ORDER:
            send(ref, ref, wz_s.at[p, k], wz_r.at[p, k], zdev(k))
        forward(p, 0)

    def take_z(p, k):
        arrived(piece(p, c, from_k(k, y)), wz_s.at[p, k], wz_r.at[p, k], zdev(k))
        forward(p, k)

    def take_y(p, k):
        ref = piece(p, c, from_k(k, 1 - y))
        arrived(ref, wy_s.at[p, k], wy_r.at[p, k], yn)
        send(ref, ref, wc_s.at[p, 4 + k], wc_r.at[p, 4 + k], sib)

    def take_core(p):
        for n, yy in ((0, y), (4, 1 - y)):
            for k in range(ZS):
                arrived(piece(p, 1 - c, from_k(k, yy)), wc_s.at[p, n + k], wc_r.at[p, n + k], sib)

    begin(0)
    activations(2)
    for n, k in enumerate(ORDER):
        take_z(0, k)
        activations(3 + n)
    begin(1)
    for n, k in enumerate((0,) + ORDER):
        take_y(0, k)
        if n < 2:
            activations(6 + n)
    take_core(0)

    block = 128

    def assemble_first(i, carry):
        at = pl.ds(pl.multiple_of(i * block, 16), block)
        even, odd = first_w[0, at, :], first_w[1, at, :]
        w_halo[at, :] = jnp.concatenate(
            [even[:, :lane], odd[:, :lane], even[:, lane:2 * lane], odd[:, lane:2 * lane]], axis=1)
        return carry

    lax.fori_loop(0, width // block, assemble_first, 0)

    chunks = 4
    size = rows // chunks

    def chunk(q):
        return pl.ds(q * size, size)

    def tap(q):
        tap_out[chunk(q), :] = product(acted[chunk(q), :], w_halo[...]).astype(jnp.bfloat16)
        send(tap_out.at[chunk(q)], tap_in.at[chunk(q)], tp_s.at[q], tp_r.at[q], xn)

    tap(0)
    tap(1)
    for k in ORDER:
        take_z(1, k)
    tap(2)
    tap(3)
    load_cot.wait()
    for k in (0,) + ORDER:
        take_y(1, k)
    take_core(1)

    def assemble_rest(i, carry):
        at = pl.ds(pl.multiple_of(i * block, 16), block)
        even, odd = rest_w[0, at, :], rest_w[1, at, :]

        def columns(m):
            return jnp.concatenate(
                [v[:, p * lane:(p + 1) * lane] for p in (m, 2 + m) for v in (even, odd)], axis=1)

        w_mid[at, :] = columns(0)
        w_point[at, :] = columns(1)
        return carry

    lax.fori_loop(0, width // block, assemble_rest, 0)

    for q in range(chunks):
        mid[chunk(q), :] = product(acted[chunk(q), :], w_mid[...])
        inner[chunk(q), :] = product(cot_ref[chunk(q), :], w_point[...])

    for q in range(chunks):
        arrived(tap_in.at[chunk(q)], tp_s.at[q], tp_r.at[q], xn)

        def one(i, carry):
            at = pl.ds(pl.multiple_of(q * size + i * step, 16), step)
            pre = mid[at, :] + tap_in[at, :].astype(jnp.float32)
            pre_out[at, :] = (inner[at, :] * gelu_slope(pre)).astype(jnp.bfloat16)
            return carry

        lax.fori_loop(0, size // step, one, 0)
        send(pre_out.at[chunk(q)], pre_in.at[chunk(q)], gp_s.at[q], gp_r.at[q], xn)

    over_rows = (((0,), (0,)), ((), ()))
    over_lanes = (((1,), (1,)), ((), ()))

    def outer(a, b):
        return lax.dot_general(a, b, over_rows, preferred_element_type=jnp.float32)

    def back(a, b):
        return lax.dot_general(a, b, over_lanes, preferred_element_type=jnp.float32)

    def share_core(t):
        def pack(start, i):
            at = pl.ds(pl.multiple_of(start + i * 64, 16), 64)
            g = grads[t, at, :] * grad_scale
            blank = jnp.zeros((64, 256 - 2 * lane), jnp.float32)

            def columns(core):
                return jnp.concatenate(
                    [g[:, p * lane:(p + 1) * lane] for p in (core, 2 + core)] + [blank], axis=1)

            even, odd = columns(0), columns(1)
            own[t, at, :] = jnp.where(c == 0, even, odd)
            sib_out[t, at, :] = jnp.where(c == 0, odd, even).astype(jnp.bfloat16)

        for k in ORDER + (0,):
            start = lax.rem(z + k, ZS) * (YS * part)
            for i in range(YS * part // 64):
                pack(start, i)
            at = pl.ds(pl.multiple_of(start, 16), YS * part)
            send(sib_out.at[t, at], sib_in.at[t, at], cs_s.at[t, k], cs_r.at[t, k], sib)

    def dest(k, yy):
        return pl.ds(pl.multiple_of((lax.rem(z + k, ZS) * YS + yy) * part, 16), part)

    def share_y(t):
        for k in ORDER + (0,):
            start = pl.multiple_of(lax.rem(z + k, ZS) * (YS * part), 16)
            arrived(sib_in.at[t, pl.ds(start, YS * part)], cs_s.at[t, k], cs_r.at[t, k], sib)
            at = dest(k, 1 - y)
            y_out[t, k] = (own[t, at, :] + sib_in[t, at, :].astype(jnp.float32)).astype(jnp.bfloat16)
            send(y_out.at[t, k], y_in.at[t, k], cy_s.at[t, k], cy_r.at[t, k], yn)

    def share_z(t):
        for k in ORDER + (0,):
            at = dest(k, y)
            arrived(y_in.at[t, k], cy_s.at[t, k], cy_r.at[t, k], yn)
            total = (own[t, at, :] + sib_in[t, at, :].astype(jnp.float32)
                     + y_in[t, k].astype(jnp.float32))
            if k:
                z_out[t, k] = total.astype(jnp.bfloat16)
                send(z_out.at[t, k], z_in.at[t, k], cz_s.at[t, k], cz_r.at[t, k], zdev(k))
            else:
                last[t] = total

    def share_x(t):
        for k in ORDER:
            arrived(z_in.at[t, k], cz_s.at[t, k], cz_r.at[t, k], zdev(k))
        total = last[t] + (z_in[t, 1].astype(jnp.float32) + z_in[t, 2].astype(jnp.float32)
                           + z_in[t, 3].astype(jnp.float32))
        last[t] = total
        x_out[t] = total.astype(jnp.bfloat16)
        send(x_out.at[t], x_in.at[t], cx_s.at[t], cx_r.at[t], xn)

    def store(q):
        return pltpu.make_async_copy(out_ref.at[chunk(q)], out_hbm.at[chunk(q)], io_s.at[2 + q])

    def finish(q):
        act = back(pre_in[chunk(q), :], w_halo[...]) + back(pre_out[chunk(q), :], w_mid[...])
        slope[chunk(q), :] = act * slope[chunk(q), :]

        def one(i, carry):
            at = pl.ds(pl.multiple_of(q * size + i * step, 16), step)
            g, n = slope[at, :], normed[at, :]
            center = jnp.mean(g * n, axis=-1, keepdims=True)
            r = scale[at, :][:, :1]
            out_ref[at, :] = (cot_ref[at, :].astype(jnp.float32) + r * (g - n * center)).astype(
                jnp.bfloat16)
            return carry

        lax.fori_loop(0, size // step, one, 0)
        store(q).start()

    def halo_term(q):
        arrived(pre_in.at[chunk(q)], gp_s.at[q], gp_r.at[q], xn)
        term = outer(acted[chunk(q), :], pre_in[chunk(q), :])
        grads[0] = term if q == 0 else grads[0] + term

    grads[1] = outer(acted[...], pre_out[...])
    share_core(1)
    share_y(1)
    halo_term(0)
    share_z(1)
    finish(0)
    halo_term(1)
    share_x(1)
    finish(1)
    halo_term(2)
    finish(2)
    halo_term(3)
    share_core(0)
    share_y(0)
    share_z(0)
    finish(3)
    share_x(0)

    def pick(v):
        return jnp.where(is_low, v[:, :lane], v[:, lane:2 * lane])

    arrived(x_in.at[1], cx_s.at[1], cx_r.at[1], xn)
    conv_ref[1] = pick(last[1]) + pick(x_in[1].astype(jnp.float32))
    arrived(x_in.at[0], cx_s.at[0], cx_r.at[0], xn)
    own_halo, their_halo = pick(last[0]), pick(x_in[0].astype(jnp.float32))
    conv_ref[0] = jnp.where(is_low, own_halo, their_halo)
    conv_ref[2] = jnp.where(is_low, their_halo, own_halo)
    for copy in pending:
        copy.wait_send()
    for q in range(chunks):
        store(q).wait()


def hand_over(grad_ref, conv_ref, grad_out, conv_out, sem):
    size = grad_ref.shape[0] // 8
    copies = [pltpu.make_async_copy(conv_ref, conv_out, sem.at[8])]
    for i in range(8):
        at = pl.ds(i * size, size)
        copies.append(pltpu.make_async_copy(grad_ref.at[at], grad_out.at[at], sem.at[i]))
    for copy in copies:
        copy.start()
    for copy in copies:
        copy.wait()


def fused_body(inputs, conv_weight, point_weight, cotangent):
    samp_count, bin_count, width = inputs.shape
    rows = samp_count * bin_count
    part = conv_weight.shape[1]
    hidden = conv_weight.shape[2] * lax.axis_size("seq")
    grad_scale = float(rows * lax.axis_size("dp") * lax.axis_size("seq")) ** (-0.5)
    bf, f32 = jnp.bfloat16, jnp.float32

    def vmem(kind, *dims):
        return pltpu.VMEM(dims, kind)

    def sems(*n):
        return [pltpu.SemaphoreType.DMA(n)] * 2

    whole = pl.BlockSpec(memory_space=pltpu.VMEM)
    away = pl.BlockSpec(memory_space=pl.ANY)
    shapes = (
        jax.ShapeDtypeStruct((rows, width), bf),
        jax.ShapeDtypeStruct(conv_weight.shape, f32),
    )
    grad, conv_grad = pl.pallas_call(
        lambda *refs: fused_kernel(grad_scale, *refs),
        out_shape=shapes,
        in_specs=[away, whole, whole, away],
        out_specs=(away, whole),
        scratch_shapes=[
            vmem(bf, rows, width), vmem(bf, rows, width), vmem(bf, rows, width),
            pltpu.SemaphoreType.DMA((6,)),
            vmem(bf, part, hidden), vmem(bf, part, hidden),
            vmem(bf, 2, width, 256), vmem(bf, 2, width, hidden),
            vmem(bf, width, hidden), vmem(bf, width, hidden), vmem(bf, width, hidden),
            vmem(bf, rows, width), vmem(f32, rows, width), vmem(f32, rows, width),
            vmem(f32, rows, 128),
            vmem(f32, rows, hidden), vmem(f32, rows, hidden), vmem(bf, rows, hidden),
            vmem(bf, rows, hidden), vmem(bf, rows, hidden), vmem(bf, rows, hidden),
            vmem(f32, 2, width, hidden), vmem(f32, 2, width, 256),
            vmem(bf, 2, width, 256), vmem(bf, 2, width, 256),
            vmem(bf, 2, 4, part, 256), vmem(bf, 2, 4, part, 256),
            vmem(bf, 2, 4, part, 256), vmem(bf, 2, 4, part, 256),
            vmem(f32, 2, part, 256), vmem(bf, 2, part, 256), vmem(bf, 2, part, 256),
            *sems(1), *sems(2, 4), *sems(2, 4), *sems(2, 8),
            *sems(4), *sems(4), *sems(2, 4), *sems(2, 4), *sems(2, 4), *sems(2),
        ],
        compiler_params=pltpu.CompilerParams(
            collective_id=0, has_side_effects=True, vmem_limit_bytes=56 * 1024 * 1024),
    )(inputs.reshape(rows, width), conv_weight, point_weight, cotangent.reshape(rows, width))
    grad, conv_grad = pl.pallas_call(
        hand_over,
        out_shape=shapes,
        in_specs=[away, away],
        out_specs=(away, away),
        scratch_shapes=[pltpu.SemaphoreType.DMA((9,))],
        compiler_params=pltpu.CompilerParams(vmem_limit_bytes=56 * 1024 * 1024),
    )(grad, conv_grad)
    return grad.reshape(samp_count, bin_count, width), conv_grad


def solution(mesh):
    return jax.shard_map(
        fused_body if fits(mesh) else body,
        mesh=mesh,
        in_specs=(P("dp", "seq", None), P(None, "dp", "seq"), P("seq", "dp"), P("dp", "seq", None)),
        out_specs=(P("dp", "seq", None), P(None, "dp", "seq")),
        check_vma=False,
    )
```
